32 devices in a mesh: blk: 8 (over z, x), head: 4 (over y, core).
Axes of the slice: x: 2, y: 2, z: 4, core: 2. Of those that a mesh axis runs over, the one named last changes fastest.
Arguments:
- qkv_rows: bfloat16 [8192, 3, 1024], P(('blk', 'head')), may hold values from -10 to 10
- neighbours: int32 [64, 32], P('blk'), may hold values from 0 to 63, as said below
- w_out: bfloat16 [1024, 1024], replicated, may hold values from -0.1875 to 0.1875
Outputs:
- projected: bfloat16 [8192, 1024], P(('blk', 'head'))
The draws below stay inside these ranges and needn't reach their ends.
Inputs may be any that keep to these rules, and one draw needn't show every extreme that they name: `neighbours`: row b lists 32 different key blocks, the first being b itself; the others lie spread over the whole sequence.
All inputs are finite; a program needn't handle non-finite values.
Results may differ from the reference program's by a relative error of at most 0.0057.
Values may be sent and summed in bfloat16 or wider, within the bound.
A program may use at most 128 MiB of HBM per device.

```python
import math
import jax
import jax.numpy as jnp
from jax import lax

HEADS = 16
HD = 64
D = 1024
BLOCK = 128
NBR = 32
TOKENS = 8192
NQB = 64


def neighbour_list(key):
    sub_key = jax.random.fold_in(key, 11)
    stride = NQB // NBR
    jitter = jax.random.randint(sub_key, (NQB, NBR), 0, stride)
    slot_ids = jnp.arange(NBR, dtype=jnp.int32)[None, :]
    offsets = jnp.where(slot_ids == 0, 0, slot_ids * stride + jitter)
    row_ids = jnp.arange(NQB, dtype=jnp.int32)[:, None]
    return ((row_ids + offsets) % NQB).astype(jnp.int32)


def draw_neighbours(key, part):
    return neighbour_list(key)


def draw_qkv_rows(key, part):
    base_key = jax.random.fold_in(key, 23)
    drawn = jnp.clip(jax.random.normal(base_key, (TOKENS, 3, D), jnp.float32), -6.0, 6.0)
    return drawn.astype(jnp.bfloat16)


def gaussian(rng, dims, width, reach, kind=jnp.bfloat16):
    array = jax.random.normal(rng, dims, jnp.float32) * width
    return jnp.minimum(jnp.maximum(array, -reach), reach).astype(kind)


def setup_inputs(seed: int = 0) -> dict:
    seeds = jax.random.split(jax.random.key(seed), 4)
    return {
        "qkv_rows": draw_qkv_rows(jax.random.fold_in(seeds[3], 71), 0),
        "neighbours": draw_neighbours(jax.random.fold_in(seeds[3], 71), 0),
        "w_out": gaussian(seeds[2], (D, D), D ** -0.5, 0.1875),
    }


def reference(qkv_rows, neighbours, w_out):
    scaling = 1.0 / math.sqrt(HD)
    queries = qkv_rows[:, 0].reshape(NQB, BLOCK, HEADS, HD)
    pairs = qkv_rows[:, 1:].reshape(NQB, BLOCK, 2, HEADS, HD)

    def attend_block(bundle):
        query_block, listed = bundle
        picked = pairs[listed]
        key_rows = picked[:, :, 0].reshape(NBR * BLOCK, HEADS, HD).astype(jnp.float32)
        value_rows = picked[:, :, 1].reshape(NBR * BLOCK, HEADS, HD).astype(jnp.float32)
        scores = jnp.einsum('qhd,khd->hqk', query_block.astype(jnp.float32), key_rows) * scaling
        scores = scores - lax.optimization_barrier(jnp.max(scores, axis=-1, keepdims=True))
        powers = jnp.exp(scores)
        weights = (powers / lax.optimization_barrier(jnp.sum(powers, axis=-1, keepdims=True))).astype(jnp.bfloat16)
        result_rows = jnp.einsum('hqk,khd->qhd', weights.astype(jnp.float32), value_rows)
        return result_rows.astype(jnp.bfloat16).reshape(BLOCK, HEADS * HD)
    attended = lax.map(attend_block, (queries, neighbours)).reshape(TOKENS, D)
    return jnp.dot(attended, w_out, preferred_element_type=jnp.float32).astype(jnp.bfloat16)
```

```python
import functools
import math

import jax
import jax.numpy as jnp
from jax import lax
from jax.experimental import pallas as pl
from jax.experimental.pallas import tpu as pltpu
from jax.sharding import PartitionSpec as P

HD = 64
BLOCK = 128
CHUNK = 4
MESH = pl.DeviceIdType.MESH
RATE = math.log2(math.e) / math.sqrt(HD)


def xor(a, b, size):
    total, bit = 0, 1
    while bit < size:
        x, y = (a // bit) % 2, (b // bit) % 2
        total = total + (x + y - 2 * x * y) * bit
        bit *= 2
    return total


def kernel(blks, slots, heads, nbr, qkv, near, out, kvp, qp, kv, qs, nbv, nbs, sbuf, mbuf, ob, att,
           kv_s, kv_r, fw_s, fw_r, nb_s, nb_r, q_s, q_r, o_s, o_r, loc):
    share = blks * slots // heads
    tokens = qkv.shape[1]
    per = tokens // BLOCK
    half = tokens // 2
    flat = lax.axis_index("blk") * slots + lax.axis_index("head")
    g, s = flat // share, flat % share

    def device(f):
        return (f // slots, f % slots)

    def peer(i):
        return xor(g, i, heads)

    def remote(src, dst, send, recv, f):
        return pltpu.make_async_remote_copy(
            src_ref=src, dst_ref=dst, send_sem=send, recv_sem=recv,
            device_id=device(f), device_id_type=MESH,
        )

    def kv_copy(i):
        p = peer(i)
        return remote(kvp.at[pl.ds(p * per, per)], kv.at[pl.ds(flat * per, per)], kv_s.at[i], kv_r.at[i],
                      p * share + s)

    def nb_copy(i):
        return remote(near, nbv.at[g], nb_s.at[i], nb_r.at[i], peer(i) * share + s)

    def q_copy(i):
        p = peer(i)
        return remote(qp.at[p], qs.at[g], q_s.at[i], q_r.at[i], p * share + s)

    def o_copy(i):
        p = peer(i)
        return remote(ob.at[p], att.at[g], o_s.at[i], o_r.at[i], p * share + s)

    def forward(i, u):
        slot = pl.ds((peer(i) * share + s) * per, per)
        return remote(kv.at[slot], kv.at[slot], fw_s.at[u - 1, i], fw_r.at[u - 1, i],
                      g * share + (s + u) % share)

    def loop(low, high, body):
        def step(t, carry):
            body(t)
            return carry
        lax.fori_loop(low, high, step, 0)

    barrier = pltpu.get_barrier_semaphore()

    def greet(t):
        pl.semaphore_signal(barrier, inc=1, device_id=device(peer(t) * share + s), device_id_type=MESH)

    loop(1, heads, greet)

    def greet_near(u):
        pl.semaphore_signal(barrier, inc=1, device_id=device(g * share + (s + u) % share), device_id_type=MESH)

    if share > 1:
        loop(1, share, greet_near)

    for h in range(heads):
        cols = slice(h * HD, (h + 1) * HD)
        kvp[h * per:(h + 1) * per] = jnp.concatenate(
            [qkv[1, :, cols], qkv[2, :, cols]], axis=1).reshape(per, BLOCK, 2 * HD)
        qp[h] = jnp.concatenate([qkv[0, :half, cols], qkv[0, half:, cols]], axis=1)
    pl.semaphore_wait(barrier, heads - 1 + share - 1)

    loop(1, heads, lambda t: kv_copy(heads - t).start())
    loop(1, heads, lambda t: nb_copy(heads - t).start())
    loop(1, heads, lambda t: q_copy(heads - t).start())
    own = [
        pltpu.make_async_copy(kvp.at[pl.ds(g * per, per)], kv.at[pl.ds(flat * per, per)], loc.at[0]),
        pltpu.make_async_copy(qp.at[g], qs.at[g], loc.at[1]),
        pltpu.make_async_copy(near, nbv.at[g], loc.at[2]),
    ]
    for copy in own:
        copy.start()
    for copy in own:
        copy.wait()

    def pass_on(i):
        if share > 1:
            loop(1, share, lambda u: forward(i, u).start())

    pass_on(0)

    def arrive(t):
        i = heads - t
        kv_copy(i).wait_recv()
        pass_on(i)

    loop(1, heads, arrive)
    loop(1, heads, lambda t: nb_copy(heads - t).wait_recv())
    table = pltpu.make_async_copy(nbv, nbs, loc.at[3])
    table.start()
    table.wait()
    if share > 1:
        loop(0, heads, lambda i: loop(1, share, lambda u: forward(i, u).wait_recv()))

    hb = per // 2
    chunks = nbr // CHUNK
    wide = CHUNK * BLOCK

    def row_of(p, b):
        return ((p * share + s) % slots) * per + b

    def query(p, b):
        rows = slice((b % hb) * BLOCK, (b % hb + 1) * BLOCK)
        lanes = slice((b // hb) * HD, (b // hb + 1) * HD)
        return jnp.concatenate([qs[p, rows, lanes], jnp.zeros((BLOCK, HD), jnp.bfloat16)], axis=1)

    def keys(p, row, c):
        return jnp.concatenate([kv[nbs[p, row, c * CHUNK + j]] for j in range(CHUNK)], axis=0)

    def scores(q, p, row, c, buf, top):
        part = lax.dot_general(q, keys(p, row, c), (((1,), (1,)), ((), ())), preferred_element_type=jnp.float32)
        sbuf[buf, :, c * wide:(c + 1) * wide] = part
        for j in range(CHUNK):
            piece = part[:, j * BLOCK:(j + 1) * BLOCK]
            top = piece if top is None else jnp.maximum(top, piece)
        return top

    def finish_top(buf, top):
        mbuf[buf] = jnp.broadcast_to(jnp.max(top, axis=1, keepdims=True), (BLOCK, BLOCK))

    def stage(buf, p, b, np_, nb_):
        row, nrow, nbuf = row_of(p, b), row_of(np_, nb_), 1 - buf
        nq = query(np_, nb_)
        top, total, acc = None, None, None
        for c in range(chunks):
            top = scores(nq, np_, nrow, c, nbuf, top)
            m = mbuf[buf]
            pieces = []
            for j in range(CHUNK):
                low = c * wide + j * BLOCK
                e = jnp.exp2((sbuf[buf, :, low:low + BLOCK] - m) * RATE)
                total = e if total is None else total + e
                pieces.append(e.astype(jnp.bfloat16))
            add = jnp.dot(jnp.concatenate(pieces, axis=1), keys(p, row, c), preferred_element_type=jnp.float32)
            acc = add if acc is None else acc + add
        finish_top(nbuf, top)
        return (acc / jnp.sum(total, axis=1, keepdims=True)).astype(jnp.bfloat16)

    top = None
    first = query(g, 0)
    for c in range(chunks):
        top = scores(first, g, row_of(g, 0), c, 0, top)
    finish_top(0, top)

    def source(t):
        i = (heads - t) % heads
        later = jnp.minimum(t + 1, heads - 1)
        ni = (heads - later) % heads
        p, np_ = peer(i), peer(ni)

        @pl.when(t + 1 < heads)
        def _():
            q_copy(ni).wait_recv()

        done = []
        for b in range(per):
            last = b == per - 1
            done.append(stage(b % 2, p, b, np_ if last else p, 0 if last else b + 1))
        for r in range(hb):
            ob[p, r * BLOCK:(r + 1) * BLOCK] = jnp.concatenate([done[r][:, HD:], done[hb + r][:, HD:]], axis=1)

        @pl.when(t > 0)
        def _():
            o_copy(i).start()

    loop(0, heads, source)
    att[g] = ob[g]
    loop(1, heads, lambda t: o_copy(heads - t).wait_recv())
    for k in range(heads // 2):
        even, odd = att[2 * k], att[2 * k + 1]
        cols = slice(2 * k * HD, (2 * k + 2) * HD)
        out[:half, cols] = jnp.concatenate([even[:, :HD], odd[:, :HD]], axis=1)
        out[half:, cols] = jnp.concatenate([even[:, HD:], odd[:, HD:]], axis=1)

    def settle(t):
        i = heads - t
        kv_copy(i).wait_send()
        nb_copy(i).wait_send()
        q_copy(i).wait_send()
        o_copy(i).wait_send()

    loop(1, heads, settle)
    if share > 1:
        loop(0, heads, lambda i: loop(1, share, lambda u: forward(i, u).wait_send()))


def solution(mesh):
    blks, slots = mesh.shape["blk"], mesh.shape["head"]

    def shards(qkv_rows, neighbours, w_out):
        tokens, _, width = qkv_rows.shape
        heads = width // HD
        share = blks * slots // heads
        per = tokens // BLOCK
        nbr = neighbours.shape[1]
        blocks = blks * slots * per
        dma = pltpu.SemaphoreType.DMA
        vmem = pl.BlockSpec(memory_space=pltpu.VMEM)
        attended = pl.pallas_call(
            functools.partial(kernel, blks, slots, heads, nbr),
            out_shape=jax.ShapeDtypeStruct((tokens, width), jnp.bfloat16),
            in_specs=[vmem, vmem],
            out_specs=vmem,
            scratch_shapes=[
                pltpu.VMEM((heads * per, BLOCK, 2 * HD), jnp.bfloat16),
                pltpu.VMEM((heads, tokens // 2, 2 * HD), jnp.bfloat16),
                pltpu.VMEM((blocks, BLOCK, 2 * HD), jnp.bfloat16),
                pltpu.VMEM((heads, tokens // 2, 2 * HD), jnp.bfloat16),
                pltpu.VMEM((heads, *neighbours.shape), jnp.int32),
                pltpu.SMEM((heads, *neighbours.shape), jnp.int32),
                pltpu.VMEM((2, BLOCK, nbr * BLOCK), jnp.float32),
                pltpu.VMEM((2, BLOCK, BLOCK), jnp.float32),
                pltpu.VMEM((heads, tokens // 2, 2 * HD), jnp.bfloat16),
                pltpu.VMEM((heads, tokens // 2, 2 * HD), jnp.bfloat16),
                dma((heads,)), dma((heads,)),
                dma((max(share - 1, 1), heads)), dma((max(share - 1, 1), heads)),
                dma((heads,)), dma((heads,)),
                dma((heads,)), dma((heads,)),
                dma((heads,)), dma((heads,)),
                dma((4,)),
            ],
            compiler_params=pltpu.CompilerParams(
                collective_id=0, has_side_effects=True, vmem_limit_bytes=48 * 2**20
            ),
        )(qkv_rows.transpose(1, 0, 2), neighbours)
        return jnp.dot(attended, w_out, preferred_element_type=jnp.float32).astype(jnp.bfloat16)

    return jax.shard_map(
        shards,
        mesh=mesh,
        in_specs=(P(("blk", "head"), None, None), P("blk", None), P()),
        out_specs=P(("blk", "head"), None),
        check_vma=False,
    )
```

```python
import functools
import math

import jax
import jax.numpy as jnp
from jax import lax
from jax.experimental import pallas as pl
from jax.experimental.pallas import tpu as pltpu
from jax.sharding import PartitionSpec as P

HD = 64
BLOCK = 128
CHUNK = 8
MESH = pl.DeviceIdType.MESH
RATE = math.log2(math.e) / math.sqrt(HD)


def xor(a, b, size):
    total, bit = 0, 1
    while bit < size:
        x, y = (a // bit) % 2, (b // bit) % 2
        total = total + (x + y - 2 * x * y) * bit
        bit *= 2
    return total


def kernel(blks, slots, heads, nbr, qkv, near, out, kp, vp, qp, kx, vt, qs, nbv, nbs, sbuf, mbuf, ob, att,
           k_s, k_r, v_s, v_r, fk_s, fk_r, fv_s, fv_r, nb_s, nb_r, q_s, q_r, o_s, o_r, loc):
    share = blks * slots // heads
    tokens = qkv.shape[1]
    per = tokens // BLOCK
    half, hb = tokens // 2, per // 2
    flat = lax.axis_index("blk") * slots + lax.axis_index("head")
    g, s = flat // share, flat % share

    def device(f):
        return (f // slots, f % slots)

    def peer(i):
        return xor(g, i, heads)

    def remote(src, dst, send, recv, f):
        return pltpu.make_async_remote_copy(
            src_ref=src, dst_ref=dst, send_sem=send, recv_sem=recv,
            device_id=device(f), device_id_type=MESH,
        )

    def k_copy(i):
        p = peer(i)
        return remote(kp.at[pl.ds(p * hb, hb)], kx.at[pl.ds(flat * per, hb)], k_s.at[i], k_r.at[i], p * share + s)

    def v_copy(i):
        p = peer(i)
        return remote(vp.at[pl.ds(p * per, per)], vt.at[pl.ds(flat * per, per)], v_s.at[i], v_r.at[i], p * share + s)

    def nb_copy(i):
        return remote(near, nbv.at[g], nb_s.at[i], nb_r.at[i], peer(i) * share + s)

    def q_copy(i):
        p = peer(i)
        return remote(qp.at[p], qs.at[g], q_s.at[i], q_r.at[i], p * share + s)

    def o_copy(i):
        p = peer(i)
        return remote(ob.at[p], att.at[g], o_s.at[i], o_r.at[i], p * share + s)

    def k_forward(i, u):
        slot = pl.ds((peer(i) * share + s) * per, hb)
        return remote(kx.at[slot], kx.at[slot], fk_s.at[u - 1, i], fk_r.at[u - 1, i], g * share + (s + u) % share)

    def v_forward(i, u):
        slot = pl.ds((peer(i) * share + s) * per, per)
        return remote(vt.at[slot], vt.at[slot], fv_s.at[u - 1, i], fv_r.at[u - 1, i], g * share + (s + u) % share)

    def loop(low, high, body):
        def step(t, carry):
            body(t)
            return carry
        if high > low:
            lax.fori_loop(low, high, step, 0)

    barrier = pltpu.get_barrier_semaphore()

    def greet(t):
        pl.semaphore_signal(barrier, inc=1, device_id=device(peer(t) * share + s), device_id_type=MESH)

    def greet_near(u):
        pl.semaphore_signal(barrier, inc=1, device_id=device(g * share + (s + u) % share), device_id_type=MESH)

    loop(1, heads, greet)
    loop(1, share, greet_near)

    def halves(part, h):
        cols = slice(h * HD, (h + 1) * HD)
        return jnp.concatenate([qkv[part, :half, cols], qkv[part, half:, cols]], axis=1)

    for h in range(heads):
        kp[h * hb:(h + 1) * hb] = halves(1, h).reshape(hb, BLOCK, 2 * HD)
    pl.semaphore_wait(barrier, heads - 1 + share - 1)
    loop(1, heads, lambda t: k_copy(heads - t).start())
    for b in range(per):
        for k in range(heads // 2):
            flipped = qkv[2, b * BLOCK:(b + 1) * BLOCK, 2 * k * HD:(2 * k + 2) * HD].T
            vp[2 * k * per + b] = flipped[:HD]
            vp[(2 * k + 1) * per + b] = flipped[HD:]
    loop(1, heads, lambda t: v_copy(heads - t).start())
    loop(1, heads, lambda t: nb_copy(heads - t).start())
    for h in range(heads):
        qp[h] = halves(0, h)
    loop(1, heads, lambda t: q_copy(heads - t).start())
    own = [
        pltpu.make_async_copy(kp.at[pl.ds(g * hb, hb)], kx.at[pl.ds(flat * per, hb)], loc.at[0]),
        pltpu.make_async_copy(vp.at[pl.ds(g * per, per)], vt.at[pl.ds(flat * per, per)], loc.at[1]),
        pltpu.make_async_copy(qp.at[g], qs.at[g], loc.at[2]),
        pltpu.make_async_copy(near, nbv.at[g], loc.at[3]),
    ]
    for copy in own:
        copy.start()
    for copy in own:
        copy.wait()

    def turn(f):
        for r in range(hb):
            x = kx[f * per + r]
            kx[f * per + hb + r] = jnp.concatenate([x[:, HD:], x[:, :HD]], axis=1)

    loop(1, share, lambda u: k_forward(0, u).start())
    loop(1, share, lambda u: v_forward(0, u).start())
    turn(flat)

    def k_arrive(t):
        i = heads - t
        k_copy(i).wait_recv()
        loop(1, share, lambda u: k_forward(i, u).start())
        turn(peer(i) * share + s)

    def v_arrive(t):
        i = heads - t
        v_copy(i).wait_recv()
        loop(1, share, lambda u: v_forward(i, u).start())

    def k_passed(t):
        i = (heads - t) % heads

        def from_near(u):
            k_forward(i, u).wait_recv()
            turn(peer(i) * share + (s + share - u) % share)

        loop(1, share, from_near)

    loop(1, heads, k_arrive)
    loop(0, heads, k_passed)
    loop(1, heads, v_arrive)
    loop(1, heads, lambda t: nb_copy(heads - t).wait_recv())
    table = pltpu.make_async_copy(nbv, nbs, loc.at[4])
    table.start()
    table.wait()
    loop(0, heads, lambda i: loop(1, share, lambda u: v_forward(i, u).wait_recv()))

    chunks = nbr // CHUNK
    pairs = CHUNK // 2
    tall = pairs * BLOCK

    def row_of(p, b):
        return ((p * share + s) % slots) * per + b

    def query(p, b):
        rows = slice((b % hb) * BLOCK, (b % hb + 1) * BLOCK)
        q = qs[p, rows, (b // hb) * HD:(b // hb + 1) * HD]
        zero = jnp.zeros((BLOCK, HD), jnp.bfloat16)
        return jnp.concatenate(
            [jnp.concatenate([q, zero], axis=1), jnp.concatenate([zero, q], axis=1)], axis=0)

    def key_pair(n, o):
        turned = (o // per) * per + (o % per + hb) % per
        return jnp.concatenate([kx[n][:, :HD], kx[turned][:, HD:]], axis=1)

    def scores(q, p, row, c, buf, top):
        keys = jnp.concatenate(
            [key_pair(nbs[p, row, c * CHUNK + 2 * j], nbs[p, row, c * CHUNK + 2 * j + 1]) for j in range(pairs)],
            axis=0)
        part = lax.dot_general(keys, q, (((1,), (1,)), ((), ())), preferred_element_type=jnp.float32)
        sbuf[buf, c * tall:(c + 1) * tall] = part
        peak = jnp.max(part.reshape(tall // 8, 8, 2 * BLOCK), axis=0)
        peak = jnp.maximum(peak[:, :BLOCK], peak[:, BLOCK:])
        return peak if top is None else jnp.maximum(top, peak)

    def finish_top(buf, top):
        mbuf[buf] = jnp.broadcast_to(jnp.max(top, axis=0, keepdims=True), (8, BLOCK))

    def stage(buf, p, b, np_, nb_):
        row, nrow, nbuf = row_of(p, b), row_of(np_, nb_), 1 - buf
        nq = query(np_, nb_)
        m = jnp.concatenate([mbuf[buf]] * 2, axis=1)
        top, total, acc = None, None, None
        for c in range(chunks):
            top = scores(nq, np_, nrow, c, nbuf, top)
            e = jnp.exp2((sbuf[buf, c * tall:(c + 1) * tall].reshape(tall // 8, 8, 2 * BLOCK) - m) * RATE)
            add = jnp.sum(e, axis=0)
            total = add if total is None else total + add
            values = jnp.concatenate(
                [jnp.concatenate([vt[nbs[p, row, c * CHUNK + 2 * j + k]] for j in range(pairs)], axis=1)
                 for k in range(2)], axis=0)
            add = jnp.dot(values, e.reshape(tall, 2 * BLOCK).astype(jnp.bfloat16),
                          preferred_element_type=jnp.float32)
            acc = add if acc is None else acc + add
        finish_top(nbuf, top)
        total = jnp.sum(total[:, :BLOCK] + total[:, BLOCK:], axis=0, keepdims=True)
        return ((acc[:HD, :BLOCK] + acc[HD:, BLOCK:]) / total).astype(jnp.bfloat16)

    top = None
    first = query(g, 0)
    for c in range(chunks):
        top = scores(first, g, row_of(g, 0), c, 0, top)
    finish_top(0, top)

    def source(t):
        i = (heads - t) % heads
        later = jnp.minimum(t + 1, heads - 1)
        ni = (heads - later) % heads
        p, np_ = peer(i), peer(ni)

        @pl.when(t + 1 < heads)
        def _():
            q_copy(ni).wait_recv()

        for b in range(per):
            last = b == per - 1
            ob[p, b] = stage(b % 2, p, b, np_ if last else p, 0 if last else b + 1)

        @pl.when(t > 0)
        def _():
            o_copy(i).start()

    loop(0, heads, source)
    att[g] = ob[g]
    loop(1, heads, lambda t: o_copy(heads - t).wait_recv())
    for h in range(heads):
        for b in range(per):
            out[h * HD:(h + 1) * HD, b * BLOCK:(b + 1) * BLOCK] = att[h, b]

    def settle(t):
        i = heads - t
        for copy in (k_copy(i), v_copy(i), nb_copy(i), q_copy(i), o_copy(i)):
            copy.wait_send()

    def settle_near(i):
        def one(u):
            k_forward(i, u).wait_send()
            v_forward(i, u).wait_send()
        loop(1, share, one)

    loop(1, heads, settle)
    loop(0, heads, settle_near)


def solution(mesh):
    blks, slots = mesh.shape["blk"], mesh.shape["head"]

    def shards(qkv_rows, neighbours, w_out):
        tokens, _, width = qkv_rows.shape
        heads = width // HD
        share = blks * slots // heads
        per = tokens // BLOCK
        nbr = neighbours.shape[1]
        blocks = blks * slots * per
        dma = pltpu.SemaphoreType.DMA
        vmem = pl.BlockSpec(memory_space=pltpu.VMEM)
        bf16, f32, i32 = jnp.bfloat16, jnp.float32, jnp.int32
        near = dma((max(share - 1, 1), heads))
        each = dma((heads,))
        attended = pl.pallas_call(
            functools.partial(kernel, blks, slots, heads, nbr),
            out_shape=jax.ShapeDtypeStruct((width, tokens), bf16),
            in_specs=[vmem, vmem],
            out_specs=vmem,
            scratch_shapes=[
                pltpu.VMEM((heads * per // 2, BLOCK, 2 * HD), bf16),
                pltpu.VMEM((heads * per, HD, BLOCK), bf16),
                pltpu.VMEM((heads, tokens // 2, 2 * HD), bf16),
                pltpu.VMEM((blocks, BLOCK, 2 * HD), bf16),
                pltpu.VMEM((blocks, HD, BLOCK), bf16),
                pltpu.VMEM((heads, tokens // 2, 2 * HD), bf16),
                pltpu.VMEM((heads, *neighbours.shape), i32),
                pltpu.SMEM((heads, *neighbours.shape), i32),
                pltpu.VMEM((2, nbr // 2 * BLOCK, 2 * BLOCK), f32),
                pltpu.VMEM((2, 8, BLOCK), f32),
                pltpu.VMEM((heads, per, HD, BLOCK), bf16),
                pltpu.VMEM((heads, per, HD, BLOCK), bf16),
                each, each, each, each, near, near, near, near, each, each, each, each, each, each,
                dma((5,)),
            ],
            compiler_params=pltpu.CompilerParams(
                collective_id=0, has_side_effects=True, vmem_limit_bytes=48 * 2**20
            ),
        )(qkv_rows.transpose(1, 0, 2), neighbours)
        return lax.dot_general(
            attended, w_out, (((0,), (0,)), ((), ())), preferred_element_type=jnp.float32
        ).astype(bf16)

    return jax.shard_map(
        shards,
        mesh=mesh,
        in_specs=(P(("blk", "head"), None, None), P("blk", None), P()),
        out_specs=P(("blk", "head"), None),
        check_vma=False,
    )
```

```python
import functools
import math

import jax
import jax.numpy as jnp
from jax import lax
from jax.experimental import pallas as pl
from jax.experimental.pallas import tpu as pltpu
from jax.sharding import PartitionSpec as P

HD = 64
BLOCK = 128
CHUNK = 8
MESH = pl.DeviceIdType.MESH
RATE = math.log2(math.e) / math.sqrt(HD)


def xor(a, b, size):
    total, bit = 0, 1
    while bit < size:
        x, y = (a // bit) % 2, (b // bit) % 2
        total = total + (x + y - 2 * x * y) * bit
        bit *= 2
    return total


def kernel(blks, slots, heads, nbr, rows, lists, out, qkv, near, kp, vp, qp, kx, vt, qs, nbv, nbs, sbuf, mbuf, ob, att,
           k_s, k_r, v_s, v_r, fk_s, fk_r, fv_s, fv_r, nb_s, nb_r, q_s, q_r, o_s, o_r, loc):
    share = blks * slots // heads
    tokens = rows.shape[1]
    per = tokens // BLOCK
    half, hb = tokens // 2, per // 2
    flat = lax.axis_index("blk") * slots + lax.axis_index("head")
    g, s = flat // share, flat % share

    def device(f):
        return (f // slots, f % slots)

    def peer(i):
        return xor(g, i, heads)

    def remote(src, dst, send, recv, f):
        return pltpu.make_async_remote_copy(
            src_ref=src, dst_ref=dst, send_sem=send, recv_sem=recv,
            device_id=device(f), device_id_type=MESH,
        )

    def k_copy(i):
        p = peer(i)
        return remote(kp.at[pl.ds(p * hb, hb)], kx.at[pl.ds(flat * per, hb)], k_s.at[i], k_r.at[i], p * share + s)

    def v_copy(i):
        p = peer(i)
        return remote(vp.at[pl.ds(p * per, per)], vt.at[pl.ds(flat * per, per)], v_s.at[i], v_r.at[i], p * share + s)

    def nb_copy(i):
        return remote(near, nbv.at[g], nb_s.at[i], nb_r.at[i], peer(i) * share + s)

    def q_copy(i):
        p = peer(i)
        return remote(qp.at[pl.ds(p * per, per)], qs.at[pl.ds(g * per, per)], q_s.at[i], q_r.at[i], p * share + s)

    def o_copy(i):
        p = peer(i)
        return remote(ob.at[p], att.at[g], o_s.at[i], o_r.at[i], p * share + s)

    def k_forward(i, u):
        slot = pl.ds((peer(i) * share + s) * per, hb)
        return remote(kx.at[slot], kx.at[slot], fk_s.at[u - 1, i], fk_r.at[u - 1, i], g * share + (s + u) % share)

    def v_forward(i, u):
        slot = pl.ds((peer(i) * share + s) * per, per)
        return remote(vt.at[slot], vt.at[slot], fv_s.at[u - 1, i], fv_r.at[u - 1, i], g * share + (s + u) % share)

    def loop(low, high, body):
        def step(t, carry):
            body(t)
            return carry
        if high > low:
            lax.fori_loop(low, high, step, 0)

    loads = [pltpu.make_async_copy(rows.at[k], qkv.at[k], loc.at[5 + k]) for k in range(3)]
    loads.append(pltpu.make_async_copy(lists, near, loc.at[8]))
    for k in (1, 2, 3, 0):
        loads[k].start()

    barrier = pltpu.get_barrier_semaphore()

    def greet(t):
        pl.semaphore_signal(barrier, inc=1, device_id=device(peer(t) * share + s), device_id_type=MESH)

    def greet_near(u):
        pl.semaphore_signal(barrier, inc=1, device_id=device(g * share + (s + u) % share), device_id_type=MESH)

    loop(1, heads, greet)
    loop(1, share, greet_near)

    loads[1].wait()
    for h in range(heads):
        cols = slice(h * HD, (h + 1) * HD)
        kp[h * hb:(h + 1) * hb] = jnp.concatenate(
            [qkv[1, :half, cols], qkv[1, half:, cols]], axis=1).reshape(hb, BLOCK, 2 * HD)
    pl.semaphore_wait(barrier, heads - 1 + share - 1)
    loop(1, heads, lambda t: k_copy(heads - t).start())

    def flip(part, target):
        loads[part].wait()
        for b in range(per):
            for k in range(heads // 2):
                flipped = qkv[part, b * BLOCK:(b + 1) * BLOCK, 2 * k * HD:(2 * k + 2) * HD].T
                target[2 * k * per + b] = flipped[:HD]
                target[(2 * k + 1) * per + b] = flipped[HD:]

    flip(2, vp)
    loop(1, heads, lambda t: v_copy(heads - t).start())
    loads[3].wait()
    loop(1, heads, lambda t: nb_copy(heads - t).start())
    flip(0, qp)
    loop(1, heads, lambda t: q_copy(heads - t).start())
    own = [
        pltpu.make_async_copy(kp.at[pl.ds(g * hb, hb)], kx.at[pl.ds(flat * per, hb)], loc.at[0]),
        pltpu.make_async_copy(vp.at[pl.ds(g * per, per)], vt.at[pl.ds(flat * per, per)], loc.at[1]),
        pltpu.make_async_copy(qp.at[pl.ds(g * per, per)], qs.at[pl.ds(g * per, per)], loc.at[2]),
        pltpu.make_async_copy(near, nbv.at[g], loc.at[3]),
    ]
    for copy in own:
        copy.start()
    for copy in own:
        copy.wait()

    def turn(f):
        for r in range(hb):
            x = kx[f * per + r]
            kx[f * per + hb + r] = jnp.concatenate([x[:, HD:], x[:, :HD]], axis=1)

    loop(1, share, lambda u: k_forward(0, u).start())
    loop(1, share, lambda u: v_forward(0, u).start())
    turn(flat)

    def k_arrive(t):
        i = heads - t
        k_copy(i).wait_recv()
        loop(1, share, lambda u: k_forward(i, u).start())
        turn(peer(i) * share + s)

    def v_arrive(t):
        i = heads - t
        v_copy(i).wait_recv()
        loop(1, share, lambda u: v_forward(i, u).start())

    def k_passed(t):
        i = (heads - t) % heads

        def from_near(u):
            k_forward(i, u).wait_recv()
            turn(peer(i) * share + (s + share - u) % share)

        loop(1, share, from_near)

    loop(1, heads, k_arrive)
    loop(0, heads, k_passed)
    loop(1, heads, v_arrive)
    loop(1, heads, lambda t: nb_copy(heads - t).wait_recv())
    table = pltpu.make_async_copy(nbv, nbs, loc.at[4])
    table.start()
    table.wait()
    loop(0, heads, lambda i: loop(1, share, lambda u: v_forward(i, u).wait_recv()))

    chunks = nbr // CHUNK
    pairs = CHUNK // 2
    tall = pairs * BLOCK

    def row_of(p, b):
        return ((p * share + s) % slots) * per + b

    def query(p, b):
        q = qs[p * per + b]
        zero = jnp.zeros((HD, BLOCK), jnp.bfloat16)
        return jnp.concatenate(
            [jnp.concatenate([q, zero], axis=1), jnp.concatenate([zero, q], axis=1)], axis=0)

    def key_pair(n, o):
        turned = (o // per) * per + (o % per + hb) % per
        return jnp.concatenate([kx[n][:, :HD], kx[turned][:, HD:]], axis=1)

    def scores(q, p, row, c, buf, top):
        keys = jnp.concatenate(
            [key_pair(nbs[p, row, c * CHUNK + 2 * j], nbs[p, row, c * CHUNK + 2 * j + 1]) for j in range(pairs)],
            axis=0)
        part = jnp.dot(keys, q, preferred_element_type=jnp.float32)
        sbuf[buf, c * tall:(c + 1) * tall] = part
        peak = jnp.max(part.reshape(tall // 64, 64, 2 * BLOCK), axis=0)
        return peak if top is None else jnp.maximum(top, peak)

    def finish_top(buf, top):
        top = jnp.max(jnp.maximum(top[:, :BLOCK], top[:, BLOCK:]), axis=0, keepdims=True)
        mbuf[buf] = jnp.broadcast_to(top, (8, BLOCK))

    def stage(buf, p, b, np_, nb_):
        row, nrow, nbuf = row_of(p, b), row_of(np_, nb_), 1 - buf
        nq = query(np_, nb_)
        m = jnp.concatenate([mbuf[buf]] * 2, axis=1)
        top, total, acc = None, None, None
        for c in range(chunks):
            top = scores(nq, np_, nrow, c, nbuf, top)
            e = jnp.exp2((sbuf[buf, c * tall:(c + 1) * tall].reshape(tall // 8, 8, 2 * BLOCK) - m) * RATE)
            add = jnp.sum(e.reshape(tall // 64, 64, 2 * BLOCK), axis=0)
            total = add if total is None else total + add
            values = jnp.concatenate(
                [jnp.concatenate([vt[nbs[p, row, c * CHUNK + 2 * j + k]] for j in range(pairs)], axis=1)
                 for k in range(2)], axis=0)
            add = jnp.dot(values, e.reshape(tall, 2 * BLOCK).astype(jnp.bfloat16),
                          preferred_element_type=jnp.float32)
            acc = add if acc is None else acc + add
        finish_top(nbuf, top)
        total = jnp.sum(total[:, :BLOCK] + total[:, BLOCK:], axis=0, keepdims=True)
        return ((acc[:HD, :BLOCK] + acc[HD:, BLOCK:]) / total).astype(jnp.bfloat16)

    top = None
    first = query(g, 0)
    for c in range(chunks):
        top = scores(first, g, row_of(g, 0), c, 0, top)
    finish_top(0, top)

    def source(t):
        i = (heads - t) % heads
        later = jnp.minimum(t + 1, heads - 1)
        ni = (heads - later) % heads
        p, np_ = peer(i), peer(ni)

        @pl.when(t + 1 < heads)
        def _():
            q_copy(ni).wait_recv()

        for b in range(per):
            last = b == per - 1
            ob[p, b] = stage(b % 2, p, b, np_ if last else p, 0 if last else b + 1)

        @pl.when(t > 0)
        def _():
            o_copy(i).start()

    loop(0, heads, source)
    att[g] = ob[g]
    loop(1, heads, lambda t: o_copy(heads - t).wait_recv())
    for h in range(heads):
        for b in range(per):
            out[h * HD:(h + 1) * HD, b * BLOCK:(b + 1) * BLOCK] = att[h, b]

    def settle(t):
        i = heads - t
        for copy in (k_copy(i), v_copy(i), nb_copy(i), q_copy(i), o_copy(i)):
            copy.wait_send()

    def settle_near(i):
        def one(u):
            k_forward(i, u).wait_send()
            v_forward(i, u).wait_send()
        loop(1, share, one)

    loop(1, heads, settle)
    loop(0, heads, settle_near)


def solution(mesh):
    blks, slots = mesh.shape["blk"], mesh.shape["head"]

    def shards(qkv_rows, neighbours, w_out):
        tokens, _, width = qkv_rows.shape
        heads = width // HD
        share = blks * slots // heads
        per = tokens // BLOCK
        nbr = neighbours.shape[1]
        blocks = blks * slots * per
        dma = pltpu.SemaphoreType.DMA
        vmem = pl.BlockSpec(memory_space=pltpu.VMEM)
        bf16, f32, i32 = jnp.bfloat16, jnp.float32, jnp.int32
        near = dma((max(share - 1, 1), heads))
        each = dma((heads,))
        attended = pl.pallas_call(
            functools.partial(kernel, blks, slots, heads, nbr),
            out_shape=jax.ShapeDtypeStruct((width, tokens), bf16),
            in_specs=[pl.BlockSpec(memory_space=pl.ANY)] * 2,
            out_specs=vmem,
            scratch_shapes=[
                pltpu.VMEM((3, tokens, width), bf16),
                pltpu.VMEM(neighbours.shape, i32),
                pltpu.VMEM((heads * per // 2, BLOCK, 2 * HD), bf16),
                pltpu.VMEM((heads * per, HD, BLOCK), bf16),
                pltpu.VMEM((heads * per, HD, BLOCK), bf16),
                pltpu.VMEM((blocks, BLOCK, 2 * HD), bf16),
                pltpu.VMEM((blocks, HD, BLOCK), bf16),
                pltpu.VMEM((heads * per, HD, BLOCK), bf16),
                pltpu.VMEM((heads, *neighbours.shape), i32),
                pltpu.SMEM((heads, *neighbours.shape), i32),
                pltpu.VMEM((2, nbr // 2 * BLOCK, 2 * BLOCK), f32),
                pltpu.VMEM((2, 8, BLOCK), f32),
                pltpu.VMEM((heads, per, HD, BLOCK), bf16),
                pltpu.VMEM((heads, per, HD, BLOCK), bf16),
                each, each, each, each, near, near, near, near, each, each, each, each, each, each,
                dma((9,)),
            ],
            compiler_params=pltpu.CompilerParams(
                collective_id=0, has_side_effects=True, vmem_limit_bytes=48 * 2**20
            ),
        )(qkv_rows.transpose(1, 0, 2), neighbours)
        return lax.dot_general(
            attended, w_out, (((0,), (0,)), ((), ())), preferred_element_type=jnp.float32
        ).astype(bf16)

    return jax.shard_map(
        shards,
        mesh=mesh,
        in_specs=(P(("blk", "head"), None, None), P("blk", None), P()),
        out_specs=P(("blk", "head"), None),
        check_vma=False,
    )
```

```python
import functools
import math

import jax
import jax.numpy as jnp
from jax import lax
from jax.experimental import pallas as pl
from jax.experimental.pallas import tpu as pltpu
from jax.sharding import PartitionSpec as P

HD = 64
BLOCK = 128
CHUNK = 8
MESH = pl.DeviceIdType.MESH
RATE = math.log2(math.e) / math.sqrt(HD)


def xor(a, b, size):
    total, bit = 0, 1
    while bit < size:
        x, y = (a // bit) % 2, (b // bit) % 2
        total = total + (x + y - 2 * x * y) * bit
        bit *= 2
    return total


def kernel(blks, slots, heads, nbr, rows, lists, out, qkv, near, kp, vp, qp, kx, vt, qs, nbv, nbs, sbuf, mbuf, ob, att,
           k_s, k_r, v_s, v_r, fk_s, fk_r, fv_s, fv_r, nb_s, nb_r, q_s, q_r, o_s, o_r, loc):
    share = blks * slots // heads
    tokens = rows.shape[1]
    per = tokens // BLOCK
    half, hb = tokens // 2, per // 2
    flat = lax.axis_index("blk") * slots + lax.axis_index("head")
    g, s = flat // share, flat % share

    def device(f):
        return (f // slots, f % slots)

    def peer(i):
        return xor(g, i, heads)

    def remote(src, dst, send, recv, f):
        return pltpu.make_async_remote_copy(
            src_ref=src, dst_ref=dst, send_sem=send, recv_sem=recv,
            device_id=device(f), device_id_type=MESH,
        )

    def order(t):
        u = jnp.maximum(t - 1, 0)
        return jnp.minimum(t, 1) * (heads - 1 - u // 2 - heads // 2 * (u % 2))

    def k_copy(i):
        p = peer(i)
        return remote(kp.at[pl.ds(p * hb, hb)], kx.at[pl.ds(flat * per, hb)], k_s.at[i], k_r.at[i], p * share + s)

    def v_copy(i):
        p = peer(i)
        return remote(vp.at[pl.ds(p * per, per)], vt.at[pl.ds(flat * per, per)], v_s.at[i], v_r.at[i], p * share + s)

    def nb_copy(i):
        return remote(near, nbv.at[g], nb_s.at[i], nb_r.at[i], peer(i) * share + s)

    def q_copy(i):
        p = peer(i)
        return remote(qp.at[pl.ds(p * per, per)], qs.at[pl.ds(g * per, per)], q_s.at[i], q_r.at[i], p * share + s)

    def o_copy(i):
        p = peer(i)
        return remote(ob.at[p], att.at[g], o_s.at[i], o_r.at[i], p * share + s)

    def k_forward(i, u):
        slot = pl.ds((peer(i) * share + s) * per, hb)
        return remote(kx.at[slot], kx.at[slot], fk_s.at[u - 1, i], fk_r.at[u - 1, i], g * share + (s + u) % share)

    def v_forward(i, u):
        slot = pl.ds((peer(i) * share + s) * per, per)
        return remote(vt.at[slot], vt.at[slot], fv_s.at[u - 1, i], fv_r.at[u - 1, i], g * share + (s + u) % share)

    def loop(low, high, body):
        def step(t, carry):
            body(t)
            return carry
        if high > low:
            lax.fori_loop(low, high, step, 0)

    loads = [pltpu.make_async_copy(rows.at[k], qkv.at[k], loc.at[5 + k]) for k in range(3)]
    loads.append(pltpu.make_async_copy(lists, near, loc.at[8]))
    for k in (1, 2, 3, 0):
        loads[k].start()

    barrier = pltpu.get_barrier_semaphore()

    def greet(t):
        pl.semaphore_signal(barrier, inc=1, device_id=device(peer(t) * share + s), device_id_type=MESH)

    def greet_near(u):
        pl.semaphore_signal(barrier, inc=1, device_id=device(g * share + (s + u) % share), device_id_type=MESH)

    loop(1, heads, greet)
    loop(1, share, greet_near)

    loads[1].wait()
    for h in range(heads):
        cols = slice(h * HD, (h + 1) * HD)
        kp[h * hb:(h + 1) * hb] = jnp.concatenate(
            [qkv[1, :half, cols], qkv[1, half:, cols]], axis=1).reshape(hb, BLOCK, 2 * HD)
    pl.semaphore_wait(barrier, heads - 1 + share - 1)
    loop(1, heads, lambda t: k_copy(order(t)).start())

    def flip(part, target):
        loads[part].wait()
        for b in range(per):
            for k in range(heads // 2):
                flipped = qkv[part, b * BLOCK:(b + 1) * BLOCK, 2 * k * HD:(2 * k + 2) * HD].T
                target[2 * k * per + b] = flipped[:HD]
                target[(2 * k + 1) * per + b] = flipped[HD:]

    flip(2, vp)
    loop(1, heads, lambda t: v_copy(order(t)).start())
    loads[3].wait()
    loop(1, heads, lambda t: nb_copy(order(t)).start())
    flip(0, qp)
    loop(1, heads, lambda t: q_copy(order(t)).start())
    own = [
        pltpu.make_async_copy(kp.at[pl.ds(g * hb, hb)], kx.at[pl.ds(flat * per, hb)], loc.at[0]),
        pltpu.make_async_copy(vp.at[pl.ds(g * per, per)], vt.at[pl.ds(flat * per, per)], loc.at[1]),
        pltpu.make_async_copy(qp.at[pl.ds(g * per, per)], qs.at[pl.ds(g * per, per)], loc.at[2]),
        pltpu.make_async_copy(near, nbv.at[g], loc.at[3]),
    ]
    for copy in own:
        copy.start()
    for copy in own:
        copy.wait()

    def turn(f):
        for r in range(hb):
            x = kx[f * per + r]
            kx[f * per + hb + r] = jnp.concatenate([x[:, HD:], x[:, :HD]], axis=1)

    loop(1, share, lambda u: k_forward(0, u).start())
    loop(1, share, lambda u: v_forward(0, u).start())
    turn(flat)

    def k_arrive(t):
        i = order(t)
        k_copy(i).wait_recv()
        loop(1, share, lambda u: k_forward(i, u).start())
        turn(peer(i) * share + s)

    def v_arrive(t):
        i = order(t)
        v_copy(i).wait_recv()
        loop(1, share, lambda u: v_forward(i, u).start())

    def k_passed(t):
        i = order(t)

        def from_near(u):
            k_forward(i, u).wait_recv()
            turn(peer(i) * share + (s + share - u) % share)

        loop(1, share, from_near)

    loop(1, heads, k_arrive)
    loop(0, heads, k_passed)
    loop(1, heads, v_arrive)
    loop(1, heads, lambda t: nb_copy(order(t)).wait_recv())
    table = pltpu.make_async_copy(nbv, nbs, loc.at[4])
    table.start()
    table.wait()
    loop(0, heads, lambda i: loop(1, share, lambda u: v_forward(i, u).wait_recv()))

    chunks = nbr // CHUNK
    pairs = CHUNK // 2
    tall = pairs * BLOCK

    def row_of(p, b):
        return ((p * share + s) % slots) * per + b

    def query(p, b):
        q = qs[p * per + b]
        zero = jnp.zeros((HD, BLOCK), jnp.bfloat16)
        return jnp.concatenate(
            [jnp.concatenate([q, zero], axis=1), jnp.concatenate([zero, q], axis=1)], axis=0)

    def key_pair(n, o):
        turned = (o // per) * per + (o % per + hb) % per
        return jnp.concatenate([kx[n][:, :HD], kx[turned][:, HD:]], axis=1)

    def scores(q, p, row, c, buf, top):
        keys = jnp.concatenate(
            [key_pair(nbs[p, row, c * CHUNK + 2 * j], nbs[p, row, c * CHUNK + 2 * j + 1]) for j in range(pairs)],
            axis=0)
        part = jnp.dot(keys, q, preferred_element_type=jnp.float32)
        sbuf[buf, c * tall:(c + 1) * tall] = part
        peak = jnp.max(part.reshape(tall // 64, 64, 2 * BLOCK), axis=0)
        return peak if top is None else jnp.maximum(top, peak)

    def finish_top(buf, top):
        top = jnp.max(jnp.maximum(top[:, :BLOCK], top[:, BLOCK:]), axis=0, keepdims=True)
        mbuf[buf] = jnp.broadcast_to(top, (8, BLOCK))

    def stage(buf, p, b, np_, nb_):
        row, nrow, nbuf = row_of(p, b), row_of(np_, nb_), 1 - buf
        nq = query(np_, nb_)
        m = jnp.concatenate([mbuf[buf]] * 2, axis=1)
        top, total, acc = None, None, None
        for c in range(chunks):
            top = scores(nq, np_, nrow, c, nbuf, top)
            e = jnp.exp2((sbuf[buf, c * tall:(c + 1) * tall].reshape(tall // 8, 8, 2 * BLOCK) - m) * RATE)
            add = jnp.sum(e.reshape(tall // 64, 64, 2 * BLOCK), axis=0)
            total = add if total is None else total + add
            values = jnp.concatenate(
                [jnp.concatenate([vt[nbs[p, row, c * CHUNK + 2 * j + k]] for j in range(pairs)], axis=1)
                 for k in range(2)], axis=0)
            add = jnp.dot(values, e.reshape(tall, 2 * BLOCK).astype(jnp.bfloat16),
                          preferred_element_type=jnp.float32)
            acc = add if acc is None else acc + add
        finish_top(nbuf, top)
        total = jnp.sum(total[:, :BLOCK] + total[:, BLOCK:], axis=0, keepdims=True)
        return ((acc[:HD, :BLOCK] + acc[HD:, BLOCK:]) / total).astype(jnp.bfloat16)

    top = None
    first = query(g, 0)
    for c in range(chunks):
        top = scores(first, g, row_of(g, 0), c, 0, top)
    finish_top(0, top)

    def source(t):
        i = order(t)
        later = jnp.minimum(t + 1, heads - 1)
        ni = order(later)
        p, np_ = peer(i), peer(ni)

        @pl.when(t + 1 < heads)
        def _():
            q_copy(ni).wait_recv()

        for b in range(per):
            last = b == per - 1
            ob[p, b] = stage(b % 2, p, b, np_ if last else p, 0 if last else b + 1)

        @pl.when(t > 0)
        def _():
            o_copy(i).start()

    loop(0, heads, source)
    att[g] = ob[g]
    loop(1, heads, lambda t: o_copy(order(t)).wait_recv())
    for h in range(heads):
        for b in range(per):
            out[h * HD:(h + 1) * HD, b * BLOCK:(b + 1) * BLOCK] = att[h, b]

    def settle(t):
        i = order(t)
        for copy in (k_copy(i), v_copy(i), nb_copy(i), q_copy(i), o_copy(i)):
            copy.wait_send()

    def settle_near(i):
        def one(u):
            k_forward(i, u).wait_send()
            v_forward(i, u).wait_send()
        loop(1, share, one)

    loop(1, heads, settle)
    loop(0, heads, settle_near)


def solution(mesh):
    blks, slots = mesh.shape["blk"], mesh.shape["head"]

    def shards(qkv_rows, neighbours, w_out):
        tokens, _, width = qkv_rows.shape
        heads = width // HD
        share = blks * slots // heads
        per = tokens // BLOCK
        nbr = neighbours.shape[1]
        blocks = blks * slots * per
        dma = pltpu.SemaphoreType.DMA
        vmem = pl.BlockSpec(memory_space=pltpu.VMEM)
        bf16, f32, i32 = jnp.bfloat16, jnp.float32, jnp.int32
        near = dma((max(share - 1, 1), heads))
        each = dma((heads,))
        attended = pl.pallas_call(
            functools.partial(kernel, blks, slots, heads, nbr),
            out_shape=jax.ShapeDtypeStruct((width, tokens), bf16),
            in_specs=[pl.BlockSpec(memory_space=pl.ANY)] * 2,
            out_specs=vmem,
            scratch_shapes=[
                pltpu.VMEM((3, tokens, width), bf16),
                pltpu.VMEM(neighbours.shape, i32),
                pltpu.VMEM((heads * per // 2, BLOCK, 2 * HD), bf16),
                pltpu.VMEM((heads * per, HD, BLOCK), bf16),
                pltpu.VMEM((heads * per, HD, BLOCK), bf16),
                pltpu.VMEM((blocks, BLOCK, 2 * HD), bf16),
                pltpu.VMEM((blocks, HD, BLOCK), bf16),
                pltpu.VMEM((heads * per, HD, BLOCK), bf16),
                pltpu.VMEM((heads, *neighbours.shape), i32),
                pltpu.SMEM((heads, *neighbours.shape), i32),
                pltpu.VMEM((2, nbr // 2 * BLOCK, 2 * BLOCK), f32),
                pltpu.VMEM((2, 8, BLOCK), f32),
                pltpu.VMEM((heads, per, HD, BLOCK), bf16),
                pltpu.VMEM((heads, per, HD, BLOCK), bf16),
                each, each, each, each, near, near, near, near, each, each, each, each, each, each,
                dma((9,)),
            ],
            compiler_params=pltpu.CompilerParams(
                collective_id=0, has_side_effects=True, vmem_limit_bytes=62 * 2**20
            ),
        )(qkv_rows.transpose(1, 0, 2), neighbours)
        return lax.dot_general(
            attended, w_out, (((0,), (0,)), ((), ())), preferred_element_type=jnp.float32
        ).astype(bf16)

    return jax.shard_map(
        shards,
        mesh=mesh,
        in_specs=(P(("blk", "head"), None, None), P("blk", None), P()),
        out_specs=P(("blk", "head"), None),
        check_vma=False,
    )
```

```python
import functools
import math

import jax
import jax.numpy as jnp
from jax import lax
from jax.experimental import pallas as pl
from jax.experimental.pallas import tpu as pltpu
from jax.sharding import PartitionSpec as P

HD = 64
BLOCK = 128
CHUNK = 8
MESH = pl.DeviceIdType.MESH
RATE = math.log2(math.e) / math.sqrt(HD)


def xor(a, b, size):
    total, bit = 0, 1
    while bit < size:
        x, y = (a // bit) % 2, (b // bit) % 2
        total = total + (x + y - 2 * x * y) * bit
        bit *= 2
    return total


def kernel(blks, slots, heads, nbr, rows, lists, out, qkv, near, kp, vp, qp, kx, vt, qs, nbv, nbs, sbuf, mbuf, pbuf, ob, att,
           k_s, k_r, v_s, v_r, fk_s, fk_r, fv_s, fv_r, nb_s, nb_r, q_s, q_r, o_s, o_r, loc):
    share = blks * slots // heads
    tokens = rows.shape[1]
    per = tokens // BLOCK
    half, hb = tokens // 2, per // 2
    flat = lax.axis_index("blk") * slots + lax.axis_index("head")
    g, s = flat // share, flat % share

    def device(f):
        return (f // slots, f % slots)

    def peer(i):
        return xor(g, i, heads)

    def remote(src, dst, send, recv, f):
        return pltpu.make_async_remote_copy(
            src_ref=src, dst_ref=dst, send_sem=send, recv_sem=recv,
            device_id=device(f), device_id_type=MESH,
        )

    def order(t):
        u = jnp.maximum(t - 1, 0)
        return jnp.minimum(t, 1) * (heads - 1 - u // 2 - heads // 2 * (u % 2))

    def k_copy(i):
        p = peer(i)
        return remote(kp.at[pl.ds(p * hb, hb)], kx.at[pl.ds(flat * per, hb)], k_s.at[i], k_r.at[i], p * share + s)

    def v_copy(i):
        p = peer(i)
        return remote(vp.at[pl.ds(p * per, per)], vt.at[pl.ds(flat * per, per)], v_s.at[i], v_r.at[i], p * share + s)

    def nb_copy(i):
        return remote(near, nbv.at[g], nb_s.at[i], nb_r.at[i], peer(i) * share + s)

    def q_copy(i):
        p = peer(i)
        return remote(qp.at[pl.ds(p * per, per)], qs.at[pl.ds(g * per, per)], q_s.at[i], q_r.at[i], p * share + s)

    def o_copy(i):
        p = peer(i)
        return remote(ob.at[pl.ds(p * per, per)], att.at[pl.ds(g * per, per)], o_s.at[i], o_r.at[i], p * share + s)

    def k_forward(i, u):
        slot = pl.ds((peer(i) * share + s) * per, hb)
        return remote(kx.at[slot], kx.at[slot], fk_s.at[u - 1, i], fk_r.at[u - 1, i], g * share + (s + u) % share)

    def v_forward(i, u):
        slot = pl.ds((peer(i) * share + s) * per, per)
        return remote(vt.at[slot], vt.at[slot], fv_s.at[u - 1, i], fv_r.at[u - 1, i], g * share + (s + u) % share)

    def loop(low, high, body):
        def step(t, carry):
            body(t)
            return carry
        if high > low:
            lax.fori_loop(low, high, step, 0)

    loads = [pltpu.make_async_copy(rows.at[k], qkv.at[k], loc.at[5 + k]) for k in range(3)]
    loads.append(pltpu.make_async_copy(lists, near, loc.at[8]))
    for k in (1, 2, 3, 0):
        loads[k].start()

    barrier = pltpu.get_barrier_semaphore()

    def greet(t):
        pl.semaphore_signal(barrier, inc=1, device_id=device(peer(t) * share + s), device_id_type=MESH)

    def greet_near(u):
        pl.semaphore_signal(barrier, inc=1, device_id=device(g * share + (s + u) % share), device_id_type=MESH)

    loop(1, heads, greet)
    loop(1, share, greet_near)

    loads[1].wait()
    for h in range(heads):
        cols = slice(h * HD, (h + 1) * HD)
        kp[h * hb:(h + 1) * hb] = jnp.concatenate(
            [qkv[1, :half, cols], qkv[1, half:, cols]], axis=1).reshape(hb, BLOCK, 2 * HD)
    pl.semaphore_wait(barrier, heads - 1 + share - 1)
    loop(1, heads, lambda t: k_copy(order(t)).start())

    def flip(part, target):
        loads[part].wait()
        for b in range(per):
            for k in range(heads // 2):
                flipped = qkv[part, b * BLOCK:(b + 1) * BLOCK, 2 * k * HD:(2 * k + 2) * HD].T
                target[2 * k * per + b] = flipped[:HD]
                target[(2 * k + 1) * per + b] = flipped[HD:]

    early = heads // 2
    loads[3].wait()
    loop(1, heads, lambda t: nb_copy(order(t)).start())
    flip(0, qp)
    loop(1, early + 1, lambda t: q_copy(order(t)).start())
    flip(2, vp)
    loop(1, heads, lambda t: v_copy(order(t)).start())
    loop(early + 1, heads, lambda t: q_copy(order(t)).start())
    own = [
        pltpu.make_async_copy(kp.at[pl.ds(g * hb, hb)], kx.at[pl.ds(flat * per, hb)], loc.at[0]),
        pltpu.make_async_copy(vp.at[pl.ds(g * per, per)], vt.at[pl.ds(flat * per, per)], loc.at[1]),
        pltpu.make_async_copy(qp.at[pl.ds(g * per, per)], qs.at[pl.ds(g * per, per)], loc.at[2]),
        pltpu.make_async_copy(near, nbv.at[g], loc.at[3]),
    ]
    for copy in own:
        copy.start()
    for copy in own:
        copy.wait()

    def turn(f):
        for r in range(hb):
            x = kx[f * per + r]
            kx[f * per + hb + r] = jnp.concatenate([x[:, HD:], x[:, :HD]], axis=1)

    loop(1, share, lambda u: k_forward(0, u).start())
    loop(1, share, lambda u: v_forward(0, u).start())
    turn(flat)

    def k_arrive(t):
        i = order(t)
        k_copy(i).wait_recv()
        loop(1, share, lambda u: k_forward(i, u).start())
        turn(peer(i) * share + s)

    def v_arrive(t):
        i = order(t)
        v_copy(i).wait_recv()
        loop(1, share, lambda u: v_forward(i, u).start())

    def k_passed(t):
        i = order(t)

        def from_near(u):
            k_forward(i, u).wait_recv()
            turn(peer(i) * share + (s + share - u) % share)

        loop(1, share, from_near)

    loop(1, heads, k_arrive)
    loop(0, heads, k_passed)
    loop(1, heads, lambda t: nb_copy(order(t)).wait_recv())
    table = pltpu.make_async_copy(nbv, nbs, loc.at[4])
    table.start()
    table.wait()
    chunks = nbr // CHUNK
    pairs = CHUNK // 2
    tall = pairs * BLOCK

    def row_of(p, b):
        return ((p * share + s) % slots) * per + b

    def query(p, b):
        q = qs[p * per + b].astype(jnp.float32) * RATE
        high = q.astype(jnp.bfloat16)
        low = (q - high.astype(jnp.float32)).astype(jnp.bfloat16)
        zero = jnp.zeros((HD, BLOCK), jnp.bfloat16)
        return jnp.concatenate(
            [jnp.concatenate(x, axis=1) for x in ((high, zero), (zero, high), (low, zero), (zero, low))], axis=0)

    def key_pair(n, o):
        turned = (o // per) * per + (o % per + hb) % per
        return jnp.concatenate([kx[n][:, :HD], kx[turned][:, HD:]], axis=1)

    def scores(q, p, row, c, buf, top):
        keys = jnp.concatenate(
            [key_pair(nbs[p, row, c * CHUNK + 2 * j], nbs[p, row, c * CHUNK + 2 * j + 1]) for j in range(pairs)],
            axis=0)
        part = jnp.dot(jnp.concatenate([keys, keys], axis=1), q, preferred_element_type=jnp.float32)
        sbuf[buf, c * tall:(c + 1) * tall] = part
        peak = jnp.max(part.reshape(tall // 64, 64, 2 * BLOCK), axis=0)
        return peak if top is None else jnp.maximum(top, peak)

    def finish_top(buf, top):
        top = jnp.max(jnp.maximum(top[:, :BLOCK], top[:, BLOCK:]), axis=0, keepdims=True)
        mbuf[buf] = jnp.broadcast_to(top, (8, BLOCK))

    def weights(buf, c):
        m = jnp.concatenate([mbuf[buf]] * 2, axis=1)
        e = jnp.exp2(sbuf[buf, c * tall:(c + 1) * tall].reshape(tall // 8, 8, 2 * BLOCK) - m)
        return e.reshape(tall, 2 * BLOCK).astype(jnp.bfloat16)

    def product(acc, p, row, c, w):
        ones = jnp.ones((16, tall), jnp.bfloat16)
        values = jnp.concatenate(
            [jnp.concatenate([vt[nbs[p, row, c * CHUNK + 2 * j + k]] for j in range(pairs)], axis=1)
             for k in range(2)] + [ones], axis=0)
        add = jnp.dot(values, w, preferred_element_type=jnp.float32)
        return add if acc is None else acc + add

    def divided(acc):
        total = acc[2 * HD:2 * HD + 1, :BLOCK] + acc[2 * HD:2 * HD + 1, BLOCK:]
        return ((acc[:HD, :BLOCK] + acc[HD:2 * HD, BLOCK:]) / total).astype(jnp.bfloat16)

    def early_stage(buf, kept, np_, nb_):
        nrow, nq, top = row_of(np_, nb_), query(np_, nb_), None
        for c in range(chunks):
            top = scores(nq, np_, nrow, c, 1 - buf, top)
            pbuf[kept, c * tall:(c + 1) * tall] = weights(buf, c)
        finish_top(1 - buf, top)

    def stage(buf, p, b, np_, nb_, op, kept):
        row, nrow, orow = row_of(p, b), row_of(np_, nb_), row_of(op, b)
        nq = query(np_, nb_)
        top, acc, old = None, None, None
        for c in range(chunks):
            top = scores(nq, np_, nrow, c, 1 - buf, top)
            old = product(old, op, orow, c, pbuf[kept, c * tall:(c + 1) * tall])
            acc = product(acc, p, row, c, weights(buf, c))
        finish_top(1 - buf, top)
        ob[p * per + b] = divided(acc)
        ob[op * per + b] = divided(old)

    top = None
    first = query(g, 0)
    for c in range(chunks):
        top = scores(first, g, row_of(g, 0), c, 0, top)
    finish_top(0, top)

    step = -(-(heads - 1) // (early - early // 2))

    def early_source(t):
        p, np_ = peer(order(t)), peer(order(t + 1))
        q_copy(order(t + 1)).wait_recv()

        @pl.when(t >= early // 2)
        def _():
            low = 1 + (t - early // 2) * step

            def body(k, carry):
                v_arrive(k)
                return carry
            lax.fori_loop(low, jnp.minimum(low + step, heads), body, 0)

        for b in range(per):
            last = b == per - 1
            early_stage(b % 2, t * per + b, np_ if last else p, 0 if last else b + 1)

    def source(t):
        later = jnp.minimum(t + 1, heads - 1)
        p, np_, op = peer(order(t)), peer(order(later)), peer(order(t - early))

        @pl.when(t + 1 < heads)
        def _():
            q_copy(order(later)).wait_recv()

        for b in range(per):
            last = b == per - 1
            stage(b % 2, p, b, np_ if last else p, 0 if last else b + 1, op, (t - early) * per + b)
        o_copy(order(t)).start()

        @pl.when(t > early)
        def _():
            o_copy(order(t - early)).start()

    loop(0, early, early_source)
    loop(0, heads, lambda i: loop(1, share, lambda u: v_forward(i, u).wait_recv()))
    loop(early, heads, source)
    for b in range(per):
        att[g * per + b] = ob[g * per + b]
    loop(1, heads, lambda t: o_copy(order(t)).wait_recv())
    for h in range(heads):
        for b in range(per):
            out[h * HD:(h + 1) * HD, b * BLOCK:(b + 1) * BLOCK] = att[h * per + b]

    def settle(t):
        i = order(t)
        for copy in (k_copy(i), v_copy(i), nb_copy(i), q_copy(i), o_copy(i)):
            copy.wait_send()

    def settle_near(i):
        def one(u):
            k_forward(i, u).wait_send()
            v_forward(i, u).wait_send()
        loop(1, share, one)

    loop(1, heads, settle)
    loop(0, heads, settle_near)


def solution(mesh):
    blks, slots = mesh.shape["blk"], mesh.shape["head"]

    def shards(qkv_rows, neighbours, w_out):
        tokens, _, width = qkv_rows.shape
        heads = width // HD
        share = blks * slots // heads
        per = tokens // BLOCK
        nbr = neighbours.shape[1]
        blocks = blks * slots * per
        dma = pltpu.SemaphoreType.DMA
        vmem = pl.BlockSpec(memory_space=pltpu.VMEM)
        bf16, f32, i32 = jnp.bfloat16, jnp.float32, jnp.int32
        near = dma((max(share - 1, 1), heads))
        each = dma((heads,))
        attended = pl.pallas_call(
            functools.partial(kernel, blks, slots, heads, nbr),
            out_shape=jax.ShapeDtypeStruct((width, tokens), bf16),
            in_specs=[pl.BlockSpec(memory_space=pl.ANY)] * 2,
            out_specs=vmem,
            scratch_shapes=[
                pltpu.VMEM((3, tokens, width), bf16),
                pltpu.VMEM(neighbours.shape, i32),
                pltpu.VMEM((heads * per // 2, BLOCK, 2 * HD), bf16),
                pltpu.VMEM((heads * per, HD, BLOCK), bf16),
                pltpu.VMEM((heads * per, HD, BLOCK), bf16),
                pltpu.VMEM((blocks, BLOCK, 2 * HD), bf16),
                pltpu.VMEM((blocks, HD, BLOCK), bf16),
                pltpu.VMEM((heads * per, HD, BLOCK), bf16),
                pltpu.VMEM((heads, *neighbours.shape), i32),
                pltpu.SMEM((heads, *neighbours.shape), i32),
                pltpu.VMEM((2, nbr // 2 * BLOCK, 2 * BLOCK), f32),
                pltpu.VMEM((2, 8, BLOCK), f32),
                pltpu.VMEM((heads // 2 * per, nbr // 2 * BLOCK, 2 * BLOCK), bf16),
                pltpu.VMEM((heads * per, HD, BLOCK), bf16),
                pltpu.VMEM((heads * per, HD, BLOCK), bf16),
                each, each, each, each, near, near, near, near, each, each, each, each, each, each,
                dma((9,)),
            ],
            compiler_params=pltpu.CompilerParams(
                collective_id=0, has_side_effects=True, vmem_limit_bytes=62 * 2**20
            ),
        )(qkv_rows.transpose(1, 0, 2), neighbours)
        return lax.dot_general(
            attended, w_out, (((0,), (0,)), ((), ())), preferred_element_type=jnp.float32
        ).astype(bf16)

    return jax.shard_map(
        shards,
        mesh=mesh,
        in_specs=(P(("blk", "head"), None, None), P("blk", None), P()),
        out_specs=P(("blk", "head"), None),
        check_vma=False,
    )
```

```python
import functools
import math

import jax
import jax.numpy as jnp
from jax import lax
from jax.experimental import pallas as pl
from jax.experimental.pallas import tpu as pltpu
from jax.sharding import PartitionSpec as P

HD = 64
BLOCK = 128
CHUNK = 8
MESH = pl.DeviceIdType.MESH
RATE = math.log2(math.e) / math.sqrt(HD)


def xor(a, b, size):
    total, bit = 0, 1
    while bit < size:
        x, y = (a // bit) % 2, (b // bit) % 2
        total = total + (x + y - 2 * x * y) * bit
        bit *= 2
    return total


def split(heads):
    late = max(heads // 4, 1)
    return heads - late, (heads - late) // late


def kernel(blks, slots, heads, nbr, rows, lists, weight, out, qkv, near, wbuf, kp, vp, qp, kx, vt, qs, nbv, nbs, sbuf, mbuf, pbuf, ob, att,
           k_s, k_r, v_s, v_r, fk_s, fk_r, fv_s, fv_r, nb_s, nb_r, q_s, q_r, o_s, o_r, loc):
    share = blks * slots // heads
    tokens = rows.shape[1]
    per = tokens // BLOCK
    half, hb = tokens // 2, per // 2
    flat = lax.axis_index("blk") * slots + lax.axis_index("head")
    g, s = flat // share, flat % share

    def device(f):
        return (f // slots, f % slots)

    def peer(i):
        return xor(g, i, heads)

    def remote(src, dst, send, recv, f):
        return pltpu.make_async_remote_copy(
            src_ref=src, dst_ref=dst, send_sem=send, recv_sem=recv,
            device_id=device(f), device_id_type=MESH,
        )

    def order(t):
        u = jnp.maximum(t - 1, 0)
        return jnp.minimum(t, 1) * (heads - 1 - u // 2 - heads // 2 * (u % 2))

    def k_copy(i):
        p = peer(i)
        return remote(kp.at[pl.ds(p * hb, hb)], kx.at[pl.ds(flat * per, hb)], k_s.at[i], k_r.at[i], p * share + s)

    def v_copy(i):
        p = peer(i)
        return remote(vp.at[pl.ds(p * per, per)], vt.at[pl.ds(flat * per, per)], v_s.at[i], v_r.at[i], p * share + s)

    def nb_copy(i):
        return remote(near, nbv.at[g], nb_s.at[i], nb_r.at[i], peer(i) * share + s)

    def q_copy(i):
        p = peer(i)
        return remote(qp.at[pl.ds(p * per, per)], qs.at[pl.ds(g * per, per)], q_s.at[i], q_r.at[i], p * share + s)

    def o_copy(i):
        p = peer(i)
        return remote(ob.at[pl.ds(p * per, per)], att.at[pl.ds(g * per, per)], o_s.at[i], o_r.at[i], p * share + s)

    def k_forward(i, u):
        slot = pl.ds((peer(i) * share + s) * per, hb)
        return remote(kx.at[slot], kx.at[slot], fk_s.at[u - 1, i], fk_r.at[u - 1, i], g * share + (s + u) % share)

    def v_forward(i, u):
        slot = pl.ds((peer(i) * share + s) * per, per)
        return remote(vt.at[slot], vt.at[slot], fv_s.at[u - 1, i], fv_r.at[u - 1, i], g * share + (s + u) % share)

    def loop(low, high, body):
        def step(t, carry):
            body(t)
            return carry
        if high > low:
            lax.fori_loop(low, high, step, 0)

    loads = [pltpu.make_async_copy(rows.at[k], qkv.at[k], loc.at[5 + k]) for k in range(3)]
    loads.append(pltpu.make_async_copy(lists, near, loc.at[8]))
    loads.append(pltpu.make_async_copy(weight, wbuf, loc.at[9]))
    for k in (1, 3, 0, 2, 4):
        loads[k].start()

    barrier = pltpu.get_barrier_semaphore()

    def greet(t):
        pl.semaphore_signal(barrier, inc=1, device_id=device(peer(t) * share + s), device_id_type=MESH)

    def greet_near(u):
        pl.semaphore_signal(barrier, inc=1, device_id=device(g * share + (s + u) % share), device_id_type=MESH)

    loop(1, heads, greet)
    loop(1, share, greet_near)

    loads[1].wait()
    for h in range(heads):
        cols = slice(h * HD, (h + 1) * HD)
        kp[h * hb:(h + 1) * hb] = jnp.concatenate(
            [qkv[1, :half, cols], qkv[1, half:, cols]], axis=1).reshape(hb, BLOCK, 2 * HD)
    pl.semaphore_wait(barrier, heads - 1 + share - 1)
    loop(1, heads, lambda t: k_copy(order(t)).start())

    def flip(part, target):
        loads[part].wait()
        for b in range(per):
            for k in range(heads // 2):
                flipped = qkv[part, b * BLOCK:(b + 1) * BLOCK, 2 * k * HD:(2 * k + 2) * HD].T
                target[2 * k * per + b] = flipped[:HD]
                target[(2 * k + 1) * per + b] = flipped[HD:]

    early, ratio = split(heads)
    loads[3].wait()
    loop(1, heads, lambda t: nb_copy(order(t)).start())
    flip(0, qp)
    loop(1, early + 1, lambda t: q_copy(order(t)).start())
    flip(2, vp)
    loop(1, heads, lambda t: v_copy(order(t)).start())
    loop(early + 1, heads, lambda t: q_copy(order(t)).start())
    own = [
        pltpu.make_async_copy(kp.at[pl.ds(g * hb, hb)], kx.at[pl.ds(flat * per, hb)], loc.at[0]),
        pltpu.make_async_copy(vp.at[pl.ds(g * per, per)], vt.at[pl.ds(flat * per, per)], loc.at[1]),
        pltpu.make_async_copy(qp.at[pl.ds(g * per, per)], qs.at[pl.ds(g * per, per)], loc.at[2]),
        pltpu.make_async_copy(near, nbv.at[g], loc.at[3]),
    ]
    for copy in own:
        copy.start()
    for copy in own:
        copy.wait()

    def turn(f):
        for r in range(hb):
            x = kx[f * per + r]
            kx[f * per + hb + r] = jnp.concatenate([x[:, HD:], x[:, :HD]], axis=1)

    loop(1, share, lambda u: k_forward(0, u).start())
    loop(1, share, lambda u: v_forward(0, u).start())
    turn(flat)

    def k_arrive(t):
        i = order(t)
        k_copy(i).wait_recv()
        loop(1, share, lambda u: k_forward(i, u).start())
        turn(peer(i) * share + s)

    def v_arrive(t):
        i = order(t)
        v_copy(i).wait_recv()
        loop(1, share, lambda u: v_forward(i, u).start())

    def k_passed(t):
        i = order(t)

        def from_near(u):
            k_forward(i, u).wait_recv()
            turn(peer(i) * share + (s + share - u) % share)

        loop(1, share, from_near)

    loop(1, heads, k_arrive)
    loop(0, heads, k_passed)
    loop(1, heads, lambda t: nb_copy(order(t)).wait_recv())
    table = pltpu.make_async_copy(nbv, nbs, loc.at[4])
    table.start()
    table.wait()
    chunks = nbr // CHUNK
    pairs = CHUNK // 2
    tall = pairs * BLOCK

    def row_of(p, b):
        return ((p * share + s) % slots) * per + b

    def query(p, b):
        q = qs[p * per + b].astype(jnp.float32) * RATE
        high = q.astype(jnp.bfloat16)
        low = (q - high.astype(jnp.float32)).astype(jnp.bfloat16)
        zero = jnp.zeros((HD, BLOCK), jnp.bfloat16)
        return jnp.concatenate(
            [jnp.concatenate(x, axis=1) for x in ((high, zero), (zero, high), (low, zero), (zero, low))], axis=0)

    def key_pair(n, o):
        turned = (o // per) * per + (o % per + hb) % per
        return jnp.concatenate([kx[n][:, :HD], kx[turned][:, HD:]], axis=1)

    def scores(q, p, row, c, buf, top):
        keys = jnp.concatenate(
            [key_pair(nbs[p, row, c * CHUNK + 2 * j], nbs[p, row, c * CHUNK + 2 * j + 1]) for j in range(pairs)],
            axis=0)
        part = jnp.dot(jnp.concatenate([keys, keys], axis=1), q, preferred_element_type=jnp.float32)
        sbuf[buf, c * tall:(c + 1) * tall] = part
        peak = jnp.max(part.reshape(tall // 64, 64, 2 * BLOCK), axis=0)
        return peak if top is None else jnp.maximum(top, peak)

    def finish_top(buf, top):
        top = jnp.max(jnp.maximum(top[:, :BLOCK], top[:, BLOCK:]), axis=0, keepdims=True)
        mbuf[buf] = jnp.broadcast_to(top, (8, BLOCK))

    def weights(buf, c):
        m = jnp.concatenate([mbuf[buf]] * 2, axis=1)
        e = jnp.exp2(sbuf[buf, c * tall:(c + 1) * tall].reshape(tall // 8, 8, 2 * BLOCK) - m)
        return e.reshape(tall, 2 * BLOCK).astype(jnp.bfloat16)

    def product(acc, p, row, c, w):
        ones = jnp.ones((16, tall), jnp.bfloat16)
        values = jnp.concatenate(
            [jnp.concatenate([vt[nbs[p, row, c * CHUNK + 2 * j + k]] for j in range(pairs)], axis=1)
             for k in range(2)] + [ones], axis=0)
        add = jnp.dot(values, w, preferred_element_type=jnp.float32)
        return add if acc is None else acc + add

    def divided(acc):
        total = acc[2 * HD:2 * HD + 1, :BLOCK] + acc[2 * HD:2 * HD + 1, BLOCK:]
        return ((acc[:HD, :BLOCK] + acc[HD:2 * HD, BLOCK:]) / total).astype(jnp.bfloat16)

    def early_stage(buf, kept, np_, nb_):
        nrow, nq, top = row_of(np_, nb_), query(np_, nb_), None
        for c in range(chunks):
            top = scores(nq, np_, nrow, c, 1 - buf, top)
            pbuf[kept, c * tall:(c + 1) * tall] = weights(buf, c)
        finish_top(1 - buf, top)

    def stage(buf, p, b, np_, nb_, old):
        row, nrow = row_of(p, b), row_of(np_, nb_)
        nq = query(np_, nb_)
        top, acc, kept = None, None, [None] * len(old)
        for c in range(chunks):
            top = scores(nq, np_, nrow, c, 1 - buf, top)
            for x, (t, op) in enumerate(old):
                kept[x] = product(kept[x], op, row_of(op, b), c, pbuf[t * per + b, c * tall:(c + 1) * tall])
            acc = product(acc, p, row, c, weights(buf, c))
        finish_top(1 - buf, top)
        for x, (t, op) in enumerate(old):
            ob[op * per + b] = divided(kept[x])
        ob[p * per + b] = divided(acc)

    top = None
    first = query(g, 0)
    for c in range(chunks):
        top = scores(first, g, row_of(g, 0), c, 0, top)
    finish_top(0, top)

    tail = max(early // 4, 1)
    step = -(-(heads - 1) // tail)

    def early_source(t):
        p, np_ = peer(order(t)), peer(order(t + 1))
        q_copy(order(t + 1)).wait_recv()

        for b in range(per):
            last = b == per - 1
            early_stage(b % 2, t * per + b, np_ if last else p, 0 if last else b + 1)

        @pl.when(t >= early - tail)
        def _():
            low = 1 + (t - (early - tail)) * step

            def body(k, carry):
                v_arrive(k)
                return carry
            lax.fori_loop(low, jnp.minimum(low + step, heads), body, 0)

    def source(t):
        later = jnp.minimum(t + 1, heads - 1)
        p, np_ = peer(order(t)), peer(order(later))
        first = (t - early) * ratio
        old = [(first + x, peer(order(first + x))) for x in range(ratio)]

        @pl.when(t + 1 < heads)
        def _():
            q_copy(order(later)).wait_recv()

        for b in range(per):
            last = b == per - 1
            stage(b % 2, p, b, np_ if last else p, 0 if last else b + 1, old)
        for x in range(ratio):
            @pl.when(first + x > 0)
            def _():
                o_copy(order(first + x)).start()
        o_copy(order(t)).start()

    loop(0, early, early_source)
    loop(0, heads, lambda i: loop(1, share, lambda u: v_forward(i, u).wait_recv()))
    loop(early, heads, source)
    for b in range(per):
        att[g * per + b] = ob[g * per + b]
    loop(1, heads, lambda t: o_copy(order(t)).wait_recv())
    loads[4].wait()
    flipped = jnp.concatenate(
        [jnp.concatenate([att[h * per + b] for b in range(per)], axis=1) for h in range(heads)], axis=0).T
    part = 2 * BLOCK
    for c in range(wbuf.shape[1] // part):
        out[:, c * part:(c + 1) * part] = jnp.dot(
            flipped, wbuf[:, c * part:(c + 1) * part], preferred_element_type=jnp.float32).astype(out.dtype)

    def settle(t):
        i = order(t)
        for copy in (k_copy(i), v_copy(i), nb_copy(i), q_copy(i), o_copy(i)):
            copy.wait_send()

    def settle_near(i):
        def one(u):
            k_forward(i, u).wait_send()
            v_forward(i, u).wait_send()
        loop(1, share, one)

    loop(1, heads, settle)
    loop(0, heads, settle_near)


def solution(mesh):
    blks, slots = mesh.shape["blk"], mesh.shape["head"]

    def shards(qkv_rows, neighbours, w_out):
        tokens, _, width = qkv_rows.shape
        heads = width // HD
        share = blks * slots // heads
        per = tokens // BLOCK
        nbr = neighbours.shape[1]
        blocks = blks * slots * per
        dma = pltpu.SemaphoreType.DMA
        vmem = pl.BlockSpec(memory_space=pltpu.VMEM)
        bf16, f32, i32 = jnp.bfloat16, jnp.float32, jnp.int32
        near = dma((max(share - 1, 1), heads))
        each = dma((heads,))
        return pl.pallas_call(
            functools.partial(kernel, blks, slots, heads, nbr),
            out_shape=jax.ShapeDtypeStruct((tokens, w_out.shape[1]), bf16),
            in_specs=[pl.BlockSpec(memory_space=pl.ANY)] * 3,
            out_specs=vmem,
            scratch_shapes=[
                pltpu.VMEM((3, tokens, width), bf16),
                pltpu.VMEM(neighbours.shape, i32),
                pltpu.VMEM(w_out.shape, bf16),
                pltpu.VMEM((heads * per // 2, BLOCK, 2 * HD), bf16),
                pltpu.VMEM((heads * per, HD, BLOCK), bf16),
                pltpu.VMEM((heads * per, HD, BLOCK), bf16),
                pltpu.VMEM((blocks, BLOCK, 2 * HD), bf16),
                pltpu.VMEM((blocks, HD, BLOCK), bf16),
                pltpu.VMEM((heads * per, HD, BLOCK), bf16),
                pltpu.VMEM((heads, *neighbours.shape), i32),
                pltpu.SMEM((heads, *neighbours.shape), i32),
                pltpu.VMEM((2, nbr // 2 * BLOCK, 2 * BLOCK), f32),
                pltpu.VMEM((2, 8, BLOCK), f32),
                pltpu.VMEM((split(heads)[0] * per, nbr // 2 * BLOCK, 2 * BLOCK), bf16),
                pltpu.VMEM((heads * per, HD, BLOCK), bf16),
                pltpu.VMEM((heads * per, HD, BLOCK), bf16),
                each, each, each, each, near, near, near, near, each, each, each, each, each, each,
                dma((10,)),
            ],
            compiler_params=pltpu.CompilerParams(
                collective_id=0, has_side_effects=True, vmem_limit_bytes=62 * 2**20
            ),
        )(qkv_rows.transpose(1, 0, 2), neighbours, w_out)

    return jax.shard_map(
        shards,
        mesh=mesh,
        in_specs=(P(("blk", "head"), None, None), P("blk", None), P()),
        out_specs=P(("blk", "head"), None),
        check_vma=False,
    )
```

```python
import functools
import math

import jax
import jax.numpy as jnp
from jax import lax
from jax.experimental import pallas as pl
from jax.experimental.pallas import tpu as pltpu
from jax.sharding import PartitionSpec as P

HD = 64
BLOCK = 128
CHUNK = 8
MESH = pl.DeviceIdType.MESH
RATE = math.log2(math.e) / math.sqrt(HD)


def xor(a, b, size):
    total, bit = 0, 1
    while bit < size:
        x, y = (a // bit) % 2, (b // bit) % 2
        total = total + (x + y - 2 * x * y) * bit
        bit *= 2
    return total


def kernel(blks, slots, heads, nbr, rows, lists, out, qkv, near, kp, vp, qp, kx, vt, qs, nbv, nbs, sbuf, mbuf, pbuf, ob, att,
           k_s, k_r, v_s, v_r, fk_s, fk_r, fv_s, fv_r, nb_s, nb_r, q_s, q_r, o_s, o_r, loc):
    share = blks * slots // heads
    tokens = rows.shape[1]
    per = tokens // BLOCK
    half, hb = tokens // 2, per // 2
    flat = lax.axis_index("blk") * slots + lax.axis_index("head")
    g, s = flat // share, flat % share

    def device(f):
        return (f // slots, f % slots)

    def peer(i):
        return xor(g, i, heads)

    def remote(src, dst, send, recv, f):
        return pltpu.make_async_remote_copy(
            src_ref=src, dst_ref=dst, send_sem=send, recv_sem=recv,
            device_id=device(f), device_id_type=MESH,
        )

    def order(t):
        u = jnp.maximum(t - 1, 0)
        return jnp.minimum(t, 1) * (heads - 1 - u // 2 - heads // 2 * (u % 2))

    def k_copy(i):
        p = peer(i)
        return remote(kp.at[pl.ds(p * hb, hb)], kx.at[pl.ds(flat * per, hb)], k_s.at[i], k_r.at[i], p * share + s)

    def v_copy(i):
        p = peer(i)
        return remote(vp.at[pl.ds(p * per, per)], vt.at[pl.ds(flat * per, per)], v_s.at[i], v_r.at[i], p * share + s)

    def nb_copy(i):
        return remote(near, nbv.at[g], nb_s.at[i], nb_r.at[i], peer(i) * share + s)

    def q_copy(i):
        p = peer(i)
        return remote(qp.at[pl.ds(p * per, per)], qs.at[pl.ds(g * per, per)], q_s.at[i], q_r.at[i], p * share + s)

    def o_copy(i):
        p = peer(i)
        return remote(ob.at[pl.ds(p * per, per)], att.at[pl.ds(g * per, per)], o_s.at[i], o_r.at[i], p * share + s)

    def k_forward(i, u):
        slot = pl.ds((peer(i) * share + s) * per, hb)
        return remote(kx.at[slot], kx.at[slot], fk_s.at[u - 1, i], fk_r.at[u - 1, i], g * share + (s + u) % share)

    def v_forward(i, u):
        slot = pl.ds((peer(i) * share + s) * per, per)
        return remote(vt.at[slot], vt.at[slot], fv_s.at[u - 1, i], fv_r.at[u - 1, i], g * share + (s + u) % share)

    def loop(low, high, body):
        def step(t, carry):
            body(t)
            return carry
        if high > low:
            lax.fori_loop(low, high, step, 0)

    loads = [pltpu.make_async_copy(rows.at[k], qkv.at[k], loc.at[5 + k]) for k in range(3)]
    loads.append(pltpu.make_async_copy(lists, near, loc.at[8]))
    for k in (1, 2, 3, 0):
        loads[k].start()

    barrier = pltpu.get_barrier_semaphore()

    def greet(t):
        pl.semaphore_signal(barrier, inc=1, device_id=device(peer(t) * share + s), device_id_type=MESH)

    def greet_near(u):
        pl.semaphore_signal(barrier, inc=1, device_id=device(g * share + (s + u) % share), device_id_type=MESH)

    loop(1, heads, greet)
    loop(1, share, greet_near)

    loads[1].wait()
    for h in range(heads):
        cols = slice(h * HD, (h + 1) * HD)
        kp[h * hb:(h + 1) * hb] = jnp.concatenate(
            [qkv[1, :half, cols], qkv[1, half:, cols]], axis=1).reshape(hb, BLOCK, 2 * HD)
    pl.semaphore_wait(barrier, heads - 1 + share - 1)
    loop(1, heads, lambda t: k_copy(order(t)).start())

    def flip(part, target):
        loads[part].wait()
        for b in range(per):
            for k in range(heads // 2):
                flipped = qkv[part, b * BLOCK:(b + 1) * BLOCK, 2 * k * HD:(2 * k + 2) * HD].T
                target[2 * k * per + b] = flipped[:HD]
                target[(2 * k + 1) * per + b] = flipped[HD:]

    early = heads // 2
    loads[3].wait()
    loop(1, heads, lambda t: nb_copy(order(t)).start())
    flip(0, qp)
    loop(1, early + 1, lambda t: q_copy(order(t)).start())
    flip(2, vp)
    loop(1, heads, lambda t: v_copy(order(t)).start())
    loop(early + 1, heads, lambda t: q_copy(order(t)).start())
    own = [
        pltpu.make_async_copy(kp.at[pl.ds(g * hb, hb)], kx.at[pl.ds(flat * per, hb)], loc.at[0]),
        pltpu.make_async_copy(vp.at[pl.ds(g * per, per)], vt.at[pl.ds(flat * per, per)], loc.at[1]),
        pltpu.make_async_copy(qp.at[pl.ds(g * per, per)], qs.at[pl.ds(g * per, per)], loc.at[2]),
        pltpu.make_async_copy(near, nbv.at[g], loc.at[3]),
    ]
    for copy in own:
        copy.start()
    for copy in own:
        copy.wait()

    def turn(f):
        for r in range(hb):
            x = kx[f * per + r]
            kx[f * per + hb + r] = jnp.concatenate([x[:, HD:], x[:, :HD]], axis=1)

    loop(1, share, lambda u: k_forward(0, u).start())
    loop(1, share, lambda u: v_forward(0, u).start())
    turn(flat)

    def k_arrive(t):
        i = order(t)
        k_copy(i).wait_recv()
        loop(1, share, lambda u: k_forward(i, u).start())
        turn(peer(i) * share + s)

    def v_arrive(t):
        i = order(t)
        v_copy(i).wait_recv()
        loop(1, share, lambda u: v_forward(i, u).start())

    def k_passed(t):
        i = order(t)

        def from_near(u):
            k_forward(i, u).wait_recv()
            turn(peer(i) * share + (s + share - u) % share)

        loop(1, share, from_near)

    loop(1, heads, k_arrive)
    loop(0, heads, k_passed)
    loop(1, heads, lambda t: nb_copy(order(t)).wait_recv())
    table = pltpu.make_async_copy(nbv, nbs, loc.at[4])
    table.start()
    table.wait()
    chunks = nbr // CHUNK
    pairs = CHUNK // 2
    tall = pairs * BLOCK

    def row_of(p, b):
        return ((p * share + s) % slots) * per + b

    def query(p, b):
        q = qs[p * per + b].astype(jnp.float32) * RATE
        high = q.astype(jnp.bfloat16)
        low = (q - high.astype(jnp.float32)).astype(jnp.bfloat16)
        zero = jnp.zeros((HD, BLOCK), jnp.bfloat16)
        return jnp.concatenate(
            [jnp.concatenate(x, axis=1) for x in ((high, zero), (zero, high), (low, zero), (zero, low))], axis=0)

    def key_pair(n, o):
        turned = (o // per) * per + (o % per + hb) % per
        return jnp.concatenate([kx[n][:, :HD], kx[turned][:, HD:]], axis=1)

    def scores(q, p, row, c, buf, top):
        keys = jnp.concatenate(
            [key_pair(nbs[p, row, c * CHUNK + 2 * j], nbs[p, row, c * CHUNK + 2 * j + 1]) for j in range(pairs)],
            axis=0)
        part = jnp.dot(jnp.concatenate([keys, keys], axis=1), q, preferred_element_type=jnp.float32)
        sbuf[buf, c * tall:(c + 1) * tall] = part
        peak = jnp.max(part.reshape(tall // 64, 64, 2 * BLOCK), axis=0)
        return peak if top is None else jnp.maximum(top, peak)

    def finish_top(buf, top):
        top = jnp.max(jnp.maximum(top[:, :BLOCK], top[:, BLOCK:]), axis=0, keepdims=True)
        mbuf[buf] = jnp.broadcast_to(top, (8, BLOCK))

    def weights(buf, c):
        m = jnp.concatenate([mbuf[buf]] * 2, axis=1)
        e = jnp.exp2(sbuf[buf, c * tall:(c + 1) * tall].reshape(tall // 8, 8, 2 * BLOCK) - m)
        return e.reshape(tall, 2 * BLOCK).astype(jnp.bfloat16)

    def product(acc, p, row, c, w):
        ones = jnp.ones((16, tall), jnp.bfloat16)
        values = jnp.concatenate(
            [jnp.concatenate([vt[nbs[p, row, c * CHUNK + 2 * j + k]] for j in range(pairs)], axis=1)
             for k in range(2)] + [ones], axis=0)
        add = jnp.dot(values, w, preferred_element_type=jnp.float32)
        return add if acc is None else acc + add

    def divided(acc):
        total = acc[2 * HD:2 * HD + 1, :BLOCK] + acc[2 * HD:2 * HD + 1, BLOCK:]
        return ((acc[:HD, :BLOCK] + acc[HD:2 * HD, BLOCK:]) / total).astype(jnp.bfloat16)

    def early_stage(buf, kept, np_, nb_):
        nrow, nq, top = row_of(np_, nb_), query(np_, nb_), None
        for c in range(chunks):
            top = scores(nq, np_, nrow, c, 1 - buf, top)
            pbuf[kept, c * tall:(c + 1) * tall] = weights(buf, c)
        finish_top(1 - buf, top)

    def stage(buf, p, b, np_, nb_, op, kept):
        row, nrow, orow = row_of(p, b), row_of(np_, nb_), row_of(op, b)
        nq = query(np_, nb_)
        top, acc, old = None, None, None
        for c in range(chunks):
            top = scores(nq, np_, nrow, c, 1 - buf, top)
            old = product(old, op, orow, c, pbuf[kept, c * tall:(c + 1) * tall])
            acc = product(acc, p, row, c, weights(buf, c))
        finish_top(1 - buf, top)
        ob[p * per + b] = divided(acc)
        ob[op * per + b] = divided(old)

    top = None
    first = query(g, 0)
    for c in range(chunks):
        top = scores(first, g, row_of(g, 0), c, 0, top)
    finish_top(0, top)

    step = -(-(heads - 1) // (early - early // 2))

    def early_source(t):
        p, np_ = peer(order(t)), peer(order(t + 1))
        q_copy(order(t + 1)).wait_recv()

        @pl.when(t >= early // 2)
        def _():
            low = 1 + (t - early // 2) * step

            def body(k, carry):
                v_arrive(k)
                return carry
            lax.fori_loop(low, jnp.minimum(low + step, heads), body, 0)

        for b in range(per):
            last = b == per - 1
            early_stage(b % 2, t * per + b, np_ if last else p, 0 if last else b + 1)

    def source(t):
        later = jnp.minimum(t + 1, heads - 1)
        p, np_, op = peer(order(t)), peer(order(later)), peer(order(t - early))

        @pl.when(t + 1 < heads)
        def _():
            q_copy(order(later)).wait_recv()

        for b in range(per):
            last = b == per - 1
            stage(b % 2, p, b, np_ if last else p, 0 if last else b + 1, op, (t - early) * per + b)
        o_copy(order(t)).start()

        @pl.when(t > early)
        def _():
            o_copy(order(t - early)).start()

    loop(0, early, early_source)
    loop(0, heads, lambda i: loop(1, share, lambda u: v_forward(i, u).wait_recv()))
    loop(early, heads, source)
    for b in range(per):
        att[g * per + b] = ob[g * per + b]
    loop(1, heads, lambda t: o_copy(order(t)).wait_recv())
    for h in range(heads):
        for b in range(per):
            out[h * HD:(h + 1) * HD, b * BLOCK:(b + 1) * BLOCK] = att[h * per + b]

    def settle(t):
        i = order(t)
        for copy in (k_copy(i), v_copy(i), nb_copy(i), q_copy(i), o_copy(i)):
            copy.wait_send()

    def settle_near(i):
        def one(u):
            k_forward(i, u).wait_send()
            v_forward(i, u).wait_send()
        loop(1, share, one)

    loop(1, heads, settle)
    loop(0, heads, settle_near)


def solution(mesh):
    blks, slots = mesh.shape["blk"], mesh.shape["head"]

    def shards(qkv_rows, neighbours, w_out):
        tokens, _, width = qkv_rows.shape
        heads = width // HD
        share = blks * slots // heads
        per = tokens // BLOCK
        nbr = neighbours.shape[1]
        blocks = blks * slots * per
        dma = pltpu.SemaphoreType.DMA
        vmem = pl.BlockSpec(memory_space=pltpu.VMEM)
        bf16, f32, i32 = jnp.bfloat16, jnp.float32, jnp.int32
        near = dma((max(share - 1, 1), heads))
        each = dma((heads,))
        attended = pl.pallas_call(
            functools.partial(kernel, blks, slots, heads, nbr),
            out_shape=jax.ShapeDtypeStruct((width, tokens), bf16),
            in_specs=[pl.BlockSpec(memory_space=pl.ANY)] * 2,
            out_specs=vmem,
            scratch_shapes=[
                pltpu.VMEM((3, tokens, width), bf16),
                pltpu.VMEM(neighbours.shape, i32),
                pltpu.VMEM((heads * per // 2, BLOCK, 2 * HD), bf16),
                pltpu.VMEM((heads * per, HD, BLOCK), bf16),
                pltpu.VMEM((heads * per, HD, BLOCK), bf16),
                pltpu.VMEM((blocks, BLOCK, 2 * HD), bf16),
                pltpu.VMEM((blocks, HD, BLOCK), bf16),
                pltpu.VMEM((heads * per, HD, BLOCK), bf16),
                pltpu.VMEM((heads, *neighbours.shape), i32),
                pltpu.SMEM((heads, *neighbours.shape), i32),
                pltpu.VMEM((2, nbr // 2 * BLOCK, 2 * BLOCK), f32),
                pltpu.VMEM((2, 8, BLOCK), f32),
                pltpu.VMEM((heads // 2 * per, nbr // 2 * BLOCK, 2 * BLOCK), bf16),
                pltpu.VMEM((heads * per, HD, BLOCK), bf16),
                pltpu.VMEM((heads * per, HD, BLOCK), bf16),
                each, each, each, each, near, near, near, near, each, each, each, each, each, each,
                dma((9,)),
            ],
            compiler_params=pltpu.CompilerParams(
                collective_id=0, has_side_effects=True, vmem_limit_bytes=121 * 2**19
            ),
        )(qkv_rows.transpose(1, 0, 2), neighbours)
        return lax.dot_general(
            attended, w_out, (((0,), (0,)), ((), ())), preferred_element_type=jnp.float32
        ).astype(bf16)

    return jax.shard_map(
        shards,
        mesh=mesh,
        in_specs=(P(("blk", "head"), None, None), P("blk", None), P()),
        out_specs=P(("blk", "head"), None),
        check_vma=False,
    )
```
